32 devices in a mesh: wide: 8 (over z, y), narrow: 4 (over x, core).
Axes of the slice: x: 2, y: 2, z: 4, core: 2. Of those that a mesh axis runs over, the one named last changes fastest.
Arguments:
- inputs: bfloat16 [32, 128, 64, 128], P(None, 'wide', 'narrow'), may hold values from -6 to 6
- cotangent: bfloat16 [32, 128, 64, 128], P(None, 'wide', 'narrow'), may hold values from -6 to 6
- active_list: int32 [8, 4, 24], P('wide', 'narrow'), may hold values from -1 to 63, as said below
- conv_first: bfloat16 [27, 32, 32], replicated, may hold values from -0.21875 to 0.21875
- conv_second: bfloat16 [27, 32, 32], replicated, may hold values from -0.21875 to 0.21875
- bias_first: float32 [32], replicated, may hold values from -4 to 4
Outputs:
- input_grad: bfloat16 [32, 128, 64, 128], P(None, 'wide', 'narrow')
- first_grad: float32 [27, 32, 32], replicated
- second_grad: float32 [27, 32, 32], replicated
- bias_grad: float32 [32], replicated
The draws below stay inside these ranges and needn't reach their ends.
Inputs may be any that keep to these rules, and one draw needn't show every extreme that they name: `active_list`: each tile's row lists distinct local block numbers of that tile in ascending order, followed by -1 in the remaining slots; every tile has one or more active blocks, and some tile has 24.
All inputs are finite; a program needn't handle non-finite values.
Results may differ from the reference program's by a relative error of at most 0.0051.
Values may be sent and summed in bfloat16 or wider, within the bound.
A program may use at most 128 MiB of HBM per device.

```python
import math
import jax
import jax.numpy as jnp
from jax import lax

C = 32
TAPS = 27
BX = 2
BY = 2
BZ = 16
CAP = 24
NX = 128
NY = 64
NZ = 128
N_WIDE = 8
N_NARROW = 4


def draw_active_list(key, part):
    block_count = BX * BY * BZ
    tile_total = N_WIDE * N_NARROW
    key_count, key_full, key_pick = jax.random.split(key, 3)
    counts = jax.random.randint(key_count, (tile_total,), 1, 2 * CAP // 3 + 1)
    full_tile = jax.random.randint(key_full, (), 0, tile_total)
    counts = jnp.where(jnp.arange(tile_total) == full_tile, CAP, counts)

    def tile_ranks(tile_key):
        return jax.random.permutation(tile_key, block_count)
    block_ranks = jax.vmap(tile_ranks)(jax.random.split(key_pick, tile_total))
    chosen = block_ranks < counts[:, None]
    block_ids = jnp.arange(block_count)
    sort_keys = jnp.where(chosen, block_ids[None, :], block_count + block_ids[None, :])
    ordering = jnp.argsort(sort_keys, axis=1)
    listed = ordering[:, :CAP]
    slot_index = jnp.arange(CAP)
    result = jnp.where(slot_index[None, :] < counts[:, None], listed, -1)
    return result.reshape(N_WIDE, N_NARROW, CAP).astype(jnp.int32)


def levels(stream_key, shape, cuts, least, top_value):
    loudness, own = 1.0, jax.random.fold_in(stream_key, 6)
    for position, blocks in cuts:
        draws = jnp.exp(jax.random.uniform(jax.random.fold_in(own, position), (blocks,), jnp.float32, least / len(cuts), top_value / len(cuts)))
        loudness = loudness * jnp.repeat(draws, shape[position] // blocks).reshape([-1 if axis == position else 1 for axis in range(len(shape))])
    return loudness


def normal_values(rng, dims, scale, reach, shards=(), kind=jnp.bfloat16):
    gain = levels(rng, dims, shards, -0.22, 0.18) if shards else 1.0
    drawn = jax.random.normal(rng, dims, jnp.float32) * scale * gain
    return jnp.minimum(jnp.maximum(drawn, -reach), reach).astype(kind)


def setup_inputs(seed: int = 0) -> dict:
    keys = jax.random.split(jax.random.key(seed), 7)
    return {
        "inputs": normal_values(keys[0], (C, NX, NY, NZ), 1.0, 6.0, ((1, 8), (2, 4))),
        "cotangent": normal_values(keys[1], (C, NX, NY, NZ), 1.0, 6.0, ((1, 8), (2, 4))),
        "active_list": draw_active_list(jax.random.fold_in(keys[6], 71), 0),
        "conv_first": normal_values(keys[3], (TAPS, C, C), (TAPS * C) ** -0.5, 0.21875),
        "conv_second": normal_values(keys[4], (TAPS, C, C), (TAPS * C) ** -0.5, 0.21875),
        "bias_first": normal_values(keys[5], (C,), 1.0, 4.0, (), jnp.float32),
    }


EDGE = 12
SPAN = 1728
WIDE_START = 157
CORE_START = 314
WIDE_LEN = 1414
CORE_LEN = 1100

def tap_offsets():
    return [da * 144 + db * 12 + dc for da in (-1, 0, 1) for db in (-1, 0, 1) for dc in (-1, 0, 1)]

def stacked_slices(source, starts, length):
    return jnp.concatenate([source[:, :, begin:begin + length] for begin in starts], axis=1)

def core_mask():
    flat_index = jnp.arange(CORE_START, CORE_START + CORE_LEN)
    plane_at = flat_index // 144
    row_at = flat_index // 12 % 12
    column_at = flat_index % 12
    inside = (plane_at >= 2) & (plane_at <= 9) & (row_at >= 2) & (row_at <= 9) & (column_at >= 2) & (column_at <= 9)
    return inside

def block_grads(window, conv_first, conv_second, bias_first):
    channels = conv_first.shape[1]
    displacements = tap_offsets()
    features = window[:, :channels].astype(jnp.float32)
    upstream = window[:, channels:2 * channels].astype(jnp.float32)
    occupied = window[:, 2 * channels:2 * channels + 1, WIDE_START:WIDE_START + WIDE_LEN].astype(jnp.float32)
    first_wide = conv_first.astype(jnp.float32)
    second_wide = conv_second.astype(jnp.float32)
    forward_matrix = jnp.transpose(first_wide, (1, 0, 2)).reshape(channels, 27 * channels)
    first_back = jnp.transpose(first_wide, (2, 0, 1)).reshape(channels, 27 * channels)
    second_back = jnp.transpose(second_wide, (2, 0, 1)).reshape(channels, 27 * channels)
    gathered_input = stacked_slices(features, [WIDE_START + step_off for step_off in displacements], WIDE_LEN)
    preact = jnp.einsum('ck,bkp->bcp', forward_matrix, gathered_input) + bias_first.astype(jnp.float32)[None, :, None]
    logistic = jax.nn.sigmoid(preact)
    hidden = (preact * logistic * occupied).astype(jnp.bfloat16)
    hidden_grad = jnp.einsum('ck,bkp->bcp', second_back, stacked_slices(upstream, [WIDE_START - step_off for step_off in displacements], WIDE_LEN))
    silu_slope = logistic * (1.0 + preact * (1.0 - logistic))
    pre_grad = (hidden_grad * silu_slope * occupied).astype(jnp.bfloat16)
    pre_wide = pre_grad.astype(jnp.float32)
    input_grad = jnp.einsum('ck,bkp->bcp', first_back, stacked_slices(pre_wide, [WIDE_START - step_off for step_off in displacements], CORE_LEN))
    core_keep = core_mask().astype(jnp.float32)
    upstream_core = upstream[:, :, CORE_START:CORE_START + CORE_LEN] * core_keep
    hidden_wide = hidden.astype(jnp.float32)
    second_grad = jnp.einsum('bjp,bkp->jk', upstream_core, stacked_slices(hidden_wide, [WIDE_START + step_off for step_off in displacements], CORE_LEN))
    pre_core = pre_wide[:, :, WIDE_START:WIDE_START + CORE_LEN] * core_keep
    first_grad = jnp.einsum('bjp,bkp->jk', pre_core, gathered_input[:, :, WIDE_START:WIDE_START + CORE_LEN])
    bias_grad = lax.optimization_barrier(jnp.sum(pre_core, axis=(0, 2)))
    batch = window.shape[0]
    input_grad = jnp.pad(input_grad, ((0, 0), (0, 0), (CORE_START, SPAN - CORE_START - CORE_LEN)))
    input_grad = input_grad.reshape(batch, channels, EDGE, EDGE, EDGE)[:, :, 2:10, 2:10, 2:10].reshape(batch, channels, 512)
    first_grad = first_grad.reshape(channels, 27, channels).transpose(1, 0, 2)
    second_grad = second_grad.reshape(channels, 27, channels).transpose(1, 0, 2)
    return (input_grad, first_grad, second_grad, bias_grad)

def reference(inputs, cotangent, active_list, conv_first, conv_second, bias_first):
    channels = inputs.shape[0]
    tiles_w, tiles_n, capacity = active_list.shape
    block_count = BX * BY * BZ
    block_ids = jnp.arange(block_count, dtype=jnp.int32)
    present = jnp.any(active_list[:, :, :, None] == block_ids[None, None, None, :], axis=2)
    present = present.reshape(tiles_w, tiles_n, BX, BY, BZ).transpose(0, 2, 1, 3, 4).reshape(tiles_w * BX, tiles_n * BY, BZ)
    cell_mask = jnp.repeat(jnp.repeat(jnp.repeat(present, 8, 0), 8, 1), 8, 2).astype(jnp.bfloat16)
    stacked = jnp.concatenate([inputs * cell_mask[None], cotangent * cell_mask[None], cell_mask[None]], axis=0)
    padded = jnp.pad(stacked, ((0, 0), (2, 2), (2, 2), (2, 2)))
    depth = stacked.shape[0]
    anchor_zero = jnp.zeros((), jnp.int32)

    def tile_step(tile_index, carried):
        tile_w = (tile_index // tiles_n).astype(jnp.int32)
        tile_n = (tile_index % tiles_n).astype(jnp.int32)
        listing = active_list[tile_w, tile_n]
        live_count = jnp.sum((listing >= 0).astype(jnp.int32))

        def block_step(slot_index, inner_carry):
            grad_grid, first_acc, second_acc, bias_acc = inner_carry
            block_id = listing[slot_index].astype(jnp.int32)
            along_x = block_id // (BY * BZ)
            along_y = block_id // BZ % BY
            along_z = block_id % BZ
            corner_x = ((tile_w * BX + along_x) * 8).astype(jnp.int32)
            corner_y = ((tile_n * BY + along_y) * 8).astype(jnp.int32)
            corner_z = (along_z * 8).astype(jnp.int32)
            window = lax.dynamic_slice(padded, (anchor_zero, corner_x, corner_y, corner_z), (depth, EDGE, EDGE, EDGE)).reshape(1, depth, SPAN)
            block_dx, first_part, second_part, bias_part = block_grads(window, conv_first, conv_second, bias_first)
            grad_grid = lax.dynamic_update_slice(grad_grid, block_dx.reshape(channels, 8, 8, 8).astype(grad_grid.dtype), (anchor_zero, corner_x, corner_y, corner_z))
            return (grad_grid, first_acc + first_part, second_acc + second_part, bias_acc + bias_part)
        return lax.fori_loop(0, live_count, block_step, carried)
    initial = (jnp.zeros(inputs.shape, jnp.float32), jnp.zeros((27, channels, channels), jnp.float32), jnp.zeros((27, channels, channels), jnp.float32), jnp.zeros((channels,), jnp.float32))
    grad_grid, first_sum, second_sum, bias_sum = lax.fori_loop(0, tiles_w * tiles_n, tile_step, initial)
    grad_scale = 1.0 / math.sqrt(NX * NY * NZ)
    return (grad_grid.astype(jnp.bfloat16), first_sum * grad_scale, second_sum * grad_scale, bias_sum * grad_scale)
```

```python
import functools
import math

import jax
import jax.numpy as jnp
from jax import lax
from jax.experimental import pallas as pl
from jax.experimental.pallas import tpu as pltpu
from jax.sharding import PartitionSpec as P

BX = 2
BY = 2
LANES = 128
GROUP = 6
WGROUP = 4


def toeplitz(taps, channels):
    kinds = taps.shape[0]
    base = taps.reshape(kinds, 3, 3, 3, channels, channels).transpose(0, 3, 4, 1, 2, 5)
    base = base.reshape(kinds, 3, channels, 3, 3 * channels)
    rows = [
        jnp.pad(base, ((0, 0),) * 4 + ((y * channels, (GROUP - 1 - y) * channels),))
        for y in range(GROUP)
    ]
    full = jnp.stack(rows, axis=2)
    return full.reshape(kinds, 3 * GROUP * channels, 3 * (GROUP + 2) * channels)


def shifted(value, step):
    lane = lax.broadcasted_iota(jnp.int32, value.shape, 1)
    moved = pltpu.roll(value, step % LANES, 1)
    return jnp.where(lane == (0 if step == 1 else LANES - 1), 0.0, moved)


def conv_rows(weights, source, row, col, channels):
    span = (GROUP + 2) * channels
    operand = jnp.concatenate(
        [source[pl.ds(row, span), pl.ds(col + p * LANES, 2 * LANES)] for p in range(3)], axis=0
    )
    out = jnp.dot(weights, operand, preferred_element_type=jnp.float32)
    m = GROUP * channels
    halves = []
    for half in range(2):
        part = out[:, half * LANES : (half + 1) * LANES]
        halves.append(
            shifted(part[:m], 1) + part[m : 2 * m] + shifted(part[2 * m :], -1)
        )
    return halves


def grads_kernel(
    channels, ny, nx,
    in_ref, cot_ref, mask_ref, xlo_ref, xhi_ref, ylo_ref, yhi_ref, w_ref, bias_ref,
    out_ref, grad_ref,
    s_in, s_cot, hid, pre, cot_sh, pre_sh, acc1, acc2, bias_acc,
):
    c = channels
    rows = ny * c
    halo = 2 * LANES
    wide = (nx + 4) * LANES
    for which, own, dst in ((0, in_ref, s_in), (1, cot_ref, s_cot)):
        for y in range(2):
            for src, at in ((ylo_ref, y), (yhi_ref, ny + 2 + y)):
                m = jnp.broadcast_to(mask_ref[at].astype(jnp.bfloat16), (c, wide))
                dst[at * c : (at + 1) * c, :] = src[(which * 2 + y) * c : (which * 2 + y + 1) * c, :] * m

        @pl.loop(0, ny)
        def _(y):
            at = pl.ds(pl.multiple_of((y + 2) * c, c), c)
            frm = pl.ds(pl.multiple_of(y * c, c), c)
            side = pl.ds(pl.multiple_of(which * rows + y * c, c), c)
            m = mask_ref[y + 2].astype(jnp.bfloat16)
            dst[at, halo : halo + nx * LANES] = own[frm, :] * jnp.broadcast_to(
                m[:, halo : halo + nx * LANES], (c, nx * LANES)
            )
            dst[at, :halo] = xlo_ref[side, :] * jnp.broadcast_to(m[:, :halo], (c, halo))
            dst[at, halo + nx * LANES :] = xhi_ref[side, :] * jnp.broadcast_to(
                m[:, halo + nx * LANES :], (c, halo)
            )

    m6 = GROUP * c
    for g in range((ny + 2) // GROUP):

        @pl.loop(0, (nx + 2) // 2)
        def _(pair):
            col = pl.multiple_of(pair * halo, halo)
            pres = conv_rows(w_ref[0], s_in, g * m6, col, c)
            backs = conv_rows(w_ref[1], s_cot, g * m6, col, c)
            for half in range(2):
                v = pres[half] + bias_ref[...]
                s = 0.5 * jnp.tanh(0.5 * v) + 0.5
                at = pl.ds(col + half * LANES, LANES)
                keep = mask_ref[g * GROUP + 1 : (g + 1) * GROUP + 1, :, pl.ds(col + (1 + half) * LANES, LANES)]
                keep = jnp.broadcast_to(keep, (GROUP, c, LANES)).reshape(m6, LANES)
                sk = s * keep
                hid[g * m6 : (g + 1) * m6, at] = (v * sk).astype(jnp.bfloat16)
                pre[g * m6 : (g + 1) * m6, at] = (
                    backs[half] * (sk * (1.0 + v * (1.0 - s)))
                ).astype(jnp.bfloat16)

    starts = list(range(0, ny - GROUP + 1, GROUP))
    if starts[-1] + GROUP < ny:
        starts.append(ny - GROUP)
    for y0 in starts:

        @pl.loop(0, nx // 2)
        def _(pair):
            col = pl.multiple_of(pair * halo, halo)
            outs = conv_rows(w_ref[2], pre, y0 * c, col, c)
            for half in range(2):
                keep = mask_ref[y0 + 2 : y0 + 2 + GROUP, :, pl.ds(col + (2 + half) * LANES, LANES)]
                keep = jnp.broadcast_to(keep, (GROUP, c, LANES)).reshape(m6, LANES)
                out_ref[y0 * c : y0 * c + m6, pl.ds(col + half * LANES, LANES)] = (
                    outs[half] * keep
                ).astype(jnp.bfloat16)

    bias_acc[...] = jnp.zeros_like(bias_acc)

    @pl.loop(0, nx)
    def _(x):
        here = pl.multiple_of(x * LANES, LANES)
        at = pl.ds(here, LANES)
        d = s_cot[2 * c : 2 * c + rows, pl.ds(here + halo, LANES)].astype(jnp.float32)
        cot_sh[0, :, at] = shifted(d, -1).astype(jnp.bfloat16)
        cot_sh[1, :, at] = shifted(d, 1).astype(jnp.bfloat16)
        p = pre[c : c + rows, pl.ds(here + LANES, LANES)].astype(jnp.float32)
        pre_sh[0, :, at] = shifted(p, -1).astype(jnp.bfloat16)
        pre_sh[1, :, at] = shifted(p, 1).astype(jnp.bfloat16)
        bias_acc[...] += jnp.sum(p.reshape(ny, c, LANES), axis=0)

    acc1[...] = jnp.zeros_like(acc1)
    acc2[...] = jnp.zeros_like(acc2)
    wr = WGROUP * c
    n = nx * LANES

    def weight_part(acc, p, y, sh, mid, mid_row, mid_col, other, other_row, other_col):
        own = pl.ds(pl.multiple_of(y * c, wr), wr)
        lhs = jnp.concatenate(
            [
                sh[0, own, :],
                mid[pl.ds(pl.multiple_of(mid_row + y * c, c), wr), mid_col : mid_col + n],
                sh[1, own, :],
            ],
            axis=0,
        )
        rhs = other[
            pl.ds(pl.multiple_of(other_row + y * c, c), (WGROUP + 2) * c),
            other_col + p * LANES : other_col + p * LANES + n,
        ]
        acc[p] += lax.dot_general(
            lhs, rhs, (((1,), (1,)), ((), ())), preferred_element_type=jnp.float32
        )

    @pl.loop(0, ny // WGROUP)
    def _(g):
        y = g * WGROUP
        for p in range(3):
            weight_part(acc1, p, y, pre_sh, pre, c, LANES, s_in, c, LANES)
            weight_part(acc2, p, y, cot_sh, s_cot, 2 * c, halo, hid, 0, 0)

    grad_ref[...] = jnp.zeros_like(grad_ref)
    for which, acc in ((0, acc1), (1, acc2)):
        for p in range(3):
            for r in range(3):
                total = acc[p, r * wr : r * wr + c, 0 : 3 * c]
                for y in range(1, WGROUP):
                    total += acc[p, r * wr + y * c : r * wr + (y + 1) * c, y * c : (y + 3) * c]
                base = ((which * 3 + p) * 3 + r) * c
                grad_ref[base : base + c, 0 : 3 * c] = total
    bias_col = jnp.sum(bias_acc[...], axis=1, keepdims=True)
    grad_ref[18 * c : 19 * c, :] = jnp.broadcast_to(bias_col, (c, LANES))


def body(inputs, cotangent, active_list, conv_first, conv_second, bias_first):
    c, nx, ny, nz = inputs.shape
    depth_blocks = nz // 8
    listing = active_list.reshape(-1)
    ids = jnp.arange(BX * BY * depth_blocks, dtype=jnp.int32)
    present = jnp.any(listing[:, None] == ids[None, :], axis=0).astype(jnp.bfloat16)
    present = present.reshape(BX, BY, depth_blocks).transpose(1, 0, 2)
    mask = jnp.repeat(jnp.repeat(jnp.repeat(present, 8, 2), 8, 1), 8, 0).reshape(ny, nx * nz)

    own_in = inputs.transpose(2, 0, 1, 3).reshape(ny * c, nx * nz)
    own_cot = cotangent.transpose(2, 0, 1, 3).reshape(ny * c, nx * nz)

    def exchange(axis, tail, head):
        count = lax.axis_size(axis)
        lo = lax.ppermute(tail, axis, [(i, i + 1) for i in range(count - 1)])
        hi = lax.ppermute(head, axis, [(i + 1, i) for i in range(count - 1)])
        return lo, hi

    w = 2 * nz
    columns = lambda cut: jnp.concatenate([cut(own_in), cut(own_cot), cut(mask)], axis=0)
    xlo, xhi = exchange(
        "wide", columns(lambda a: a[:, -w:]), columns(lambda a: a[:, :w])
    )
    n = ny * c

    def rows(first):
        parts = []
        for base, own, per in ((0, own_in, c), (n, own_cot, c), (2 * n, mask, 1)):
            r0 = 0 if first else (ny - 2) * per
            r1 = r0 + 2 * per
            parts.append(
                jnp.concatenate(
                    [xlo[base + r0 : base + r1], own[r0:r1], xhi[base + r0 : base + r1]], axis=1
                )
            )
        return jnp.concatenate(parts, axis=0)

    ylo, yhi = exchange("narrow", rows(False), rows(True))
    mask_mid = jnp.concatenate([xlo[2 * n :], mask, xhi[2 * n :]], axis=1)
    full_mask = jnp.concatenate([ylo[4 * c :], mask_mid, yhi[4 * c :]], axis=0)
    full_mask = full_mask.astype(jnp.float32).reshape(ny + 4, 1, (nx + 4) * nz)

    taps = jnp.stack(
        [
            conv_first,
            conv_second[::-1].transpose(0, 2, 1),
            conv_first[::-1].transpose(0, 2, 1),
        ]
    )
    weights = toeplitz(taps, c)
    bias = jnp.broadcast_to(bias_first[None, :, None], (GROUP, c, LANES)).reshape(-1, LANES)

    vmem = pl.BlockSpec(memory_space=pltpu.VMEM)
    bf = jnp.bfloat16
    out, grads = pl.pallas_call(
        functools.partial(grads_kernel, c, ny, nx),
        out_shape=(
            jax.ShapeDtypeStruct((ny * c, nx * nz), bf),
            jax.ShapeDtypeStruct((19 * c, LANES), jnp.float32),
        ),
        in_specs=[vmem] * 9,
        out_specs=(vmem, vmem),
        scratch_shapes=[
            pltpu.VMEM(((ny + 4) * c, (nx + 4) * nz), bf),
            pltpu.VMEM(((ny + 4) * c, (nx + 4) * nz), bf),
            pltpu.VMEM(((ny + 2) * c, (nx + 2) * nz), bf),
            pltpu.VMEM(((ny + 2) * c, (nx + 2) * nz), bf),
            pltpu.VMEM((2, ny * c, nx * nz), bf),
            pltpu.VMEM((2, ny * c, nx * nz), bf),
            pltpu.VMEM((3, 3 * WGROUP * c, (WGROUP + 2) * c), jnp.float32),
            pltpu.VMEM((3, 3 * WGROUP * c, (WGROUP + 2) * c), jnp.float32),
            pltpu.VMEM((c, LANES), jnp.float32),
        ],
        compiler_params=pltpu.CompilerParams(vmem_limit_bytes=56 * 1024 * 1024),
        name="local_grads",
    )(own_in, own_cot, full_mask, xlo[: 2 * n], xhi[: 2 * n], ylo[: 4 * c], yhi[: 4 * c], weights, bias)

    input_grad = out.reshape(ny, c, nx, nz).transpose(1, 2, 0, 3)
    scale = 1.0 / math.sqrt(nx * lax.axis_size("wide") * ny * lax.axis_size("narrow") * nz)
    grads = lax.psum(grads, ("wide", "narrow")) * scale
    both = grads[: 18 * c, : 3 * c].reshape(2, 3, 3, c, 3, c).transpose(0, 1, 4, 2, 3, 5)
    both = both.reshape(2, 27, c, c)
    return input_grad, both[0], both[1], grads[18 * c :, 0]


def solution(mesh):
    return jax.shard_map(
        body,
        mesh=mesh,
        in_specs=(
            P(None, "wide", "narrow", None),
            P(None, "wide", "narrow", None),
            P("wide", "narrow", None),
            P(),
            P(),
            P(),
        ),
        out_specs=(P(None, "wide", "narrow", None), P(), P(), P()),
        check_vma=False,
    )
```

```python
import functools
import math

import jax
import jax.numpy as jnp
from jax import lax
from jax.experimental import pallas as pl
from jax.experimental.pallas import tpu as pltpu
from jax.sharding import PartitionSpec as P

BX = 2
BY = 2
LANES = 128
GROUP = 6
WGROUP = 4


def toeplitz(taps, channels):
    kinds = taps.shape[0]
    base = taps.reshape(kinds, 3, 3, 3, channels, channels).transpose(0, 3, 4, 1, 2, 5)
    base = base.reshape(kinds, 3, channels, 3, 3 * channels)
    rows = [
        jnp.pad(base, ((0, 0),) * 4 + ((y * channels, (GROUP - 1 - y) * channels),))
        for y in range(GROUP)
    ]
    full = jnp.stack(rows, axis=2)
    return full.reshape(kinds, 3 * GROUP * channels, 3 * (GROUP + 2) * channels)


def shifted(value, step):
    lane = lax.broadcasted_iota(jnp.int32, value.shape, 1)
    moved = pltpu.roll(value, step % LANES, 1)
    return jnp.where(lane == (0 if step == 1 else LANES - 1), 0.0, moved)


def conv_rows(weights, source, row, col, channels):
    span = (GROUP + 2) * channels
    operand = jnp.concatenate(
        [source[pl.ds(row, span), pl.ds(col + p * LANES, 2 * LANES)] for p in range(3)], axis=0
    )
    out = jnp.dot(weights, operand, preferred_element_type=jnp.float32)
    m = GROUP * channels
    halves = []
    for half in range(2):
        part = out[:, half * LANES : (half + 1) * LANES]
        halves.append(
            shifted(part[:m], 1) + part[m : 2 * m] + shifted(part[2 * m :], -1)
        )
    return halves


def grads_kernel(
    channels, ny, nx,
    in_ref, cot_ref, mask_ref, xlo_ref, xhi_ref, ylo_ref, yhi_ref, w_ref, bias_ref,
    out_ref, grad_ref,
    s_in, s_cot, hid, pre, cot_sh, pre_sh, acc1, acc2, bias_acc,
):
    c = channels
    rows = ny * c
    halo = 2 * LANES
    wide = (nx + 4) * LANES
    for which, own, dst in ((0, in_ref, s_in), (1, cot_ref, s_cot)):
        for y in range(2):
            for src, at in ((ylo_ref, y), (yhi_ref, ny + 2 + y)):
                m = jnp.broadcast_to(mask_ref[at].astype(jnp.bfloat16), (c, wide))
                dst[at * c : (at + 1) * c, :] = src[(which * 2 + y) * c : (which * 2 + y + 1) * c, :] * m

        @pl.loop(0, ny)
        def _(y):
            at = pl.ds(pl.multiple_of((y + 2) * c, c), c)
            frm = pl.ds(pl.multiple_of(y * c, c), c)
            side = pl.ds(pl.multiple_of(which * rows + y * c, c), c)
            m = mask_ref[y + 2].astype(jnp.bfloat16)
            dst[at, halo : halo + nx * LANES] = own[frm, :] * jnp.broadcast_to(
                m[:, halo : halo + nx * LANES], (c, nx * LANES)
            )
            dst[at, :halo] = xlo_ref[side, :] * jnp.broadcast_to(m[:, :halo], (c, halo))
            dst[at, halo + nx * LANES :] = xhi_ref[side, :] * jnp.broadcast_to(
                m[:, halo + nx * LANES :], (c, halo)
            )

    m6 = GROUP * c
    for g in range((ny + 2) // GROUP):

        @pl.loop(0, (nx + 2) // 2)
        def _(pair):
            col = pl.multiple_of(pair * halo, halo)
            pres = conv_rows(w_ref[0], s_in, g * m6, col, c)
            backs = conv_rows(w_ref[1], s_cot, g * m6, col, c)
            for half in range(2):
                v = pres[half] + bias_ref[...]
                s = 0.5 * jnp.tanh(0.5 * v) + 0.5
                at = pl.ds(col + half * LANES, LANES)
                keep = mask_ref[g * GROUP + 1 : (g + 1) * GROUP + 1, :, pl.ds(col + (1 + half) * LANES, LANES)]
                keep = jnp.broadcast_to(keep, (GROUP, c, LANES)).reshape(m6, LANES)
                sk = s * keep
                hid[g * m6 : (g + 1) * m6, at] = (v * sk).astype(jnp.bfloat16)
                pre[g * m6 : (g + 1) * m6, at] = (
                    backs[half] * (sk * (1.0 + v * (1.0 - s)))
                ).astype(jnp.bfloat16)

    starts = list(range(0, ny - GROUP + 1, GROUP))
    if starts[-1] + GROUP < ny:
        starts.append(ny - GROUP)
    for y0 in starts:

        @pl.loop(0, nx // 2)
        def _(pair):
            col = pl.multiple_of(pair * halo, halo)
            outs = conv_rows(w_ref[2], pre, y0 * c, col, c)
            for half in range(2):
                keep = mask_ref[y0 + 2 : y0 + 2 + GROUP, :, pl.ds(col + (2 + half) * LANES, LANES)]
                keep = jnp.broadcast_to(keep, (GROUP, c, LANES)).reshape(m6, LANES)
                out_ref[y0 * c : y0 * c + m6, pl.ds(col + half * LANES, LANES)] = (
                    outs[half] * keep
                ).astype(jnp.bfloat16)

    bias_acc[...] = jnp.zeros_like(bias_acc)

    @pl.loop(0, nx)
    def _(x):
        here = pl.multiple_of(x * LANES, LANES)
        at = pl.ds(here, LANES)
        d = s_cot[2 * c : 2 * c + rows, pl.ds(here + halo, LANES)].astype(jnp.float32)
        cot_sh[0, :, at] = shifted(d, -1).astype(jnp.bfloat16)
        cot_sh[1, :, at] = shifted(d, 1).astype(jnp.bfloat16)
        p = pre[c : c + rows, pl.ds(here + LANES, LANES)].astype(jnp.float32)
        pre_sh[0, :, at] = shifted(p, -1).astype(jnp.bfloat16)
        pre_sh[1, :, at] = shifted(p, 1).astype(jnp.bfloat16)
        bias_acc[...] += jnp.sum(p.reshape(ny, c, LANES), axis=0)

    acc1[...] = jnp.zeros_like(acc1)
    acc2[...] = jnp.zeros_like(acc2)
    wr = WGROUP * c
    n = nx * LANES

    def weight_part(acc, p, y, sh, mid, mid_row, mid_col, other, other_row, other_col):
        own = pl.ds(pl.multiple_of(y * c, wr), wr)
        lhs = jnp.concatenate(
            [
                sh[0, own, :],
                mid[pl.ds(pl.multiple_of(mid_row + y * c, c), wr), mid_col : mid_col + n],
                sh[1, own, :],
            ],
            axis=0,
        )
        rhs = other[
            pl.ds(pl.multiple_of(other_row + y * c, c), (WGROUP + 2) * c),
            other_col + p * LANES : other_col + p * LANES + n,
        ]
        acc[p] += lax.dot_general(
            lhs, rhs, (((1,), (1,)), ((), ())), preferred_element_type=jnp.float32
        )

    @pl.loop(0, ny // WGROUP)
    def _(g):
        y = g * WGROUP
        for p in range(3):
            weight_part(acc1, p, y, pre_sh, pre, c, LANES, s_in, c, LANES)
            weight_part(acc2, p, y, cot_sh, s_cot, 2 * c, halo, hid, 0, 0)

    grad_ref[...] = jnp.zeros_like(grad_ref)
    for which, acc in ((0, acc1), (1, acc2)):
        for p in range(3):
            for r in range(3):
                total = acc[p, r * wr : r * wr + c, 0 : 3 * c]
                for y in range(1, WGROUP):
                    total += acc[p, r * wr + y * c : r * wr + (y + 1) * c, y * c : (y + 3) * c]
                base = ((which * 3 + p) * 3 + r) * c
                grad_ref[base : base + c, 0 : 3 * c] = total
    bias_col = jnp.sum(bias_acc[...], axis=1, keepdims=True)
    grad_ref[:c, 3 * c :] = jnp.broadcast_to(bias_col, (c, LANES - 3 * c))


def total_kernel(
    wide, narrow, scale, x_ref, out_ref,
    part, parts_n, parts_w, block, whole,
    s1, r1, s2, r2, s3, r3, s4, r4,
):
    me_w, me_n = lax.axis_index("wide"), lax.axis_index("narrow")

    def send(src, dst, s, r, w, n):
        copy = pltpu.make_async_remote_copy(
            src_ref=src, dst_ref=dst, send_sem=s, recv_sem=r,
            device_id=(w, n), device_id_type=pl.DeviceIdType.MESH,
        )
        copy.start()
        return copy

    barrier = pltpu.get_barrier_semaphore()
    peers_n = [lax.rem(me_n + k, narrow) for k in range(1, narrow)]
    peers_w = [lax.rem(me_w + k, wide) for k in range(1, wide)]
    for n in peers_n:
        pl.semaphore_signal(barrier, inc=1, device_id=(me_w, n), device_id_type=pl.DeviceIdType.MESH)
    for w in peers_w:
        pl.semaphore_signal(barrier, inc=1, device_id=(w, me_n), device_id_type=pl.DeviceIdType.MESH)
    pl.semaphore_wait(barrier, len(peers_n) + len(peers_w))

    copies = [
        send(x_ref.at[n], parts_n.at[k], s1.at[k], r1.at[k], me_w, n)
        for k, n in enumerate(peers_n)
    ]
    for copy in copies:
        copy.wait()
    total = x_ref[me_n]
    for k in range(narrow - 1):
        total += parts_n[k]
    part[...] = total
    copies = [
        send(part.at[w], parts_w.at[k], s2.at[k], r2.at[k], w, me_n)
        for k, w in enumerate(peers_w)
    ]
    for copy in copies:
        copy.wait()
    total = part[me_w]
    for k in range(wide - 1):
        total += parts_w[k]
    block[me_w] = total * scale
    copies = [
        send(block.at[me_w], block.at[me_w], s3.at[k], r3.at[k], w, me_n)
        for k, w in enumerate(peers_w)
    ]
    for copy in copies:
        copy.wait()
    whole[me_n] = block[...]
    copies = [
        send(block, whole.at[me_n], s4.at[k], r4.at[k], me_w, n)
        for k, n in enumerate(peers_n)
    ]
    for copy in copies:
        copy.wait()
    out_ref[...] = whole[...]


def total(grads, wide, narrow, scale):
    lanes = grads.shape[-1]
    rows = grads.shape[0] // (wide * narrow)
    vmem = pl.BlockSpec(memory_space=pltpu.VMEM)
    f32 = jnp.float32
    sems = [
        pltpu.SemaphoreType.DMA((count - 1,))
        for count in (narrow, narrow, wide, wide, wide, wide, narrow, narrow)
    ]
    out = pl.pallas_call(
        functools.partial(total_kernel, wide, narrow, scale),
        out_shape=jax.ShapeDtypeStruct((narrow, wide, rows, lanes), f32),
        in_specs=[vmem],
        out_specs=vmem,
        scratch_shapes=[
            pltpu.VMEM((wide, rows, lanes), f32),
            pltpu.VMEM((narrow - 1, wide, rows, lanes), f32),
            pltpu.VMEM((wide - 1, rows, lanes), f32),
            pltpu.VMEM((wide, rows, lanes), f32),
            pltpu.VMEM((narrow, wide, rows, lanes), f32),
        ] + sems,
        compiler_params=pltpu.CompilerParams(collective_id=0, has_side_effects=True),
        name="total",
    )(grads.reshape(narrow, wide, rows, lanes))
    return out.reshape(-1, lanes)


def body(inputs, cotangent, active_list, conv_first, conv_second, bias_first):
    c, nx, ny, nz = inputs.shape
    depth_blocks = nz // 8
    listing = active_list.reshape(-1)
    ids = jnp.arange(BX * BY * depth_blocks, dtype=jnp.int32)
    present = jnp.any(listing[:, None] == ids[None, :], axis=0).astype(jnp.bfloat16)
    present = present.reshape(BX, BY, depth_blocks).transpose(1, 0, 2)
    mask = jnp.repeat(jnp.repeat(jnp.repeat(present, 8, 2), 8, 1), 8, 0).reshape(ny, nx * nz)

    own_in = inputs.transpose(2, 0, 1, 3).reshape(ny * c, nx * nz)
    own_cot = cotangent.transpose(2, 0, 1, 3).reshape(ny * c, nx * nz)

    def exchange(axis, tail, head):
        count = lax.axis_size(axis)
        lo = lax.ppermute(tail, axis, [(i, i + 1) for i in range(count - 1)])
        hi = lax.ppermute(head, axis, [(i + 1, i) for i in range(count - 1)])
        return lo, hi

    w = 2 * nz
    columns = lambda cut: jnp.concatenate([cut(own_in), cut(own_cot), cut(mask)], axis=0)
    xlo, xhi = exchange(
        "wide", columns(lambda a: a[:, -w:]), columns(lambda a: a[:, :w])
    )
    n = ny * c

    def rows(first):
        parts = []
        for base, own, per in ((0, own_in, c), (n, own_cot, c), (2 * n, mask, 1)):
            r0 = 0 if first else (ny - 2) * per
            r1 = r0 + 2 * per
            parts.append(
                jnp.concatenate(
                    [xlo[base + r0 : base + r1], own[r0:r1], xhi[base + r0 : base + r1]], axis=1
                )
            )
        return jnp.concatenate(parts, axis=0)

    ylo, yhi = exchange("narrow", rows(False), rows(True))
    mask_mid = jnp.concatenate([xlo[2 * n :], mask, xhi[2 * n :]], axis=1)
    full_mask = jnp.concatenate([ylo[4 * c :], mask_mid, yhi[4 * c :]], axis=0)
    full_mask = full_mask.astype(jnp.float32).reshape(ny + 4, 1, (nx + 4) * nz)

    taps = jnp.stack(
        [
            conv_first,
            conv_second[::-1].transpose(0, 2, 1),
            conv_first[::-1].transpose(0, 2, 1),
        ]
    )
    weights = toeplitz(taps, c)
    bias = jnp.broadcast_to(bias_first[None, :, None], (GROUP, c, LANES)).reshape(-1, LANES)

    wide, narrow = lax.axis_size("wide"), lax.axis_size("narrow")
    unit = wide * narrow * 8
    grad_rows = -(-18 * c // unit) * unit
    vmem = pl.BlockSpec(memory_space=pltpu.VMEM)
    bf = jnp.bfloat16
    out, grads = pl.pallas_call(
        functools.partial(grads_kernel, c, ny, nx),
        out_shape=(
            jax.ShapeDtypeStruct((ny * c, nx * nz), bf),
            jax.ShapeDtypeStruct((grad_rows, LANES), jnp.float32),
        ),
        in_specs=[vmem] * 9,
        out_specs=(vmem, vmem),
        scratch_shapes=[
            pltpu.VMEM(((ny + 4) * c, (nx + 4) * nz), bf),
            pltpu.VMEM(((ny + 4) * c, (nx + 4) * nz), bf),
            pltpu.VMEM(((ny + 2) * c, (nx + 2) * nz), bf),
            pltpu.VMEM(((ny + 2) * c, (nx + 2) * nz), bf),
            pltpu.VMEM((2, ny * c, nx * nz), bf),
            pltpu.VMEM((2, ny * c, nx * nz), bf),
            pltpu.VMEM((3, 3 * WGROUP * c, (WGROUP + 2) * c), jnp.float32),
            pltpu.VMEM((3, 3 * WGROUP * c, (WGROUP + 2) * c), jnp.float32),
            pltpu.VMEM((c, LANES), jnp.float32),
        ],
        compiler_params=pltpu.CompilerParams(vmem_limit_bytes=56 * 1024 * 1024),
        name="local_grads",
    )(own_in, own_cot, full_mask, xlo[: 2 * n], xhi[: 2 * n], ylo[: 4 * c], yhi[: 4 * c], weights, bias)

    input_grad = out.reshape(ny, c, nx, nz).transpose(1, 2, 0, 3)
    scale = 1.0 / math.sqrt(nx * wide * ny * narrow * nz)
    grads = total(grads, wide, narrow, scale)
    both = grads[: 18 * c, : 3 * c].reshape(2, 3, 3, c, 3, c).transpose(0, 1, 4, 2, 3, 5)
    both = both.reshape(2, 27, c, c)
    return input_grad, both[0], both[1], grads[:c, 3 * c]


def solution(mesh):
    return jax.shard_map(
        body,
        mesh=mesh,
        in_specs=(
            P(None, "wide", "narrow", None),
            P(None, "wide", "narrow", None),
            P("wide", "narrow", None),
            P(),
            P(),
            P(),
        ),
        out_specs=(P(None, "wide", "narrow", None), P(), P(), P()),
        check_vma=False,
    )
```

```python
import functools
import math

import jax
import jax.numpy as jnp
from jax import lax
from jax.experimental import pallas as pl
from jax.experimental.pallas import tpu as pltpu
from jax.sharding import PartitionSpec as P

BX = 2
BY = 2
LANES = 128
GROUP = 6
WGROUP = 4


def toeplitz(taps, channels):
    kinds = taps.shape[0]
    base = taps.reshape(kinds, 3, 3, 3, channels, channels).transpose(0, 3, 4, 1, 2, 5)
    base = base.reshape(kinds, 3, channels, 3, 3 * channels)
    rows = [
        jnp.pad(base, ((0, 0),) * 4 + ((y * channels, (GROUP - 1 - y) * channels),))
        for y in range(GROUP)
    ]
    full = jnp.stack(rows, axis=2)
    return full.reshape(kinds, 3 * GROUP * channels, 3 * (GROUP + 2) * channels)


def shifted(value, step):
    lane = lax.broadcasted_iota(jnp.int32, value.shape, 1)
    moved = pltpu.roll(value, step % LANES, 1)
    return jnp.where(lane == (0 if step == 1 else LANES - 1), 0.0, moved)


def conv_rows(weights, source, row, col, channels):
    span = (GROUP + 2) * channels
    operand = jnp.concatenate(
        [source[pl.ds(row, span), pl.ds(col + p * LANES, 2 * LANES)] for p in range(3)], axis=0
    )
    out = jnp.dot(weights, operand, preferred_element_type=jnp.float32)
    m = GROUP * channels
    halves = []
    for half in range(2):
        part = out[:, half * LANES : (half + 1) * LANES]
        halves.append(
            shifted(part[:m], 1) + part[m : 2 * m] + shifted(part[2 * m :], -1)
        )
    return halves


def row_starts(ny):
    starts = list(range(0, ny - GROUP + 1, GROUP))
    if starts[-1] + GROUP < ny:
        starts.append(ny - GROUP)
    return starts


def keep_rows(mask_ref, row, col, channels):
    keep = mask_ref[row : row + GROUP, :, pl.ds(col, LANES)]
    return jnp.broadcast_to(keep, (GROUP, channels, LANES)).reshape(GROUP * channels, LANES)


def grads_kernel(
    channels, ny, nx,
    in_ref, cot_ref, mask_ref, xlo_ref, xhi_ref, ylo_ref, yhi_ref, w_ref, bias_ref,
    pre_ref, grad_ref,
    s_in, s_cot, hid, hid_sh, pre_sh, acc1, acc2, bias_acc,
):
    c = channels
    rows = ny * c
    n = nx * LANES
    wide = n + 2 * LANES
    for which, own, dst in ((0, in_ref, s_in), (1, cot_ref, s_cot)):
        for src, at in ((ylo_ref, 0), (yhi_ref, ny + 1)):
            m = jnp.broadcast_to(mask_ref[at].astype(jnp.bfloat16), (c, wide))
            dst[at * c : (at + 1) * c, :] = src[which * c : (which + 1) * c, :] * m

        @pl.loop(0, ny)
        def _(y):
            at = pl.ds(pl.multiple_of((y + 1) * c, c), c)
            frm = pl.ds(pl.multiple_of(y * c, c), c)
            side = pl.ds(pl.multiple_of(which * rows + y * c, c), c)
            m = mask_ref[y + 1].astype(jnp.bfloat16)
            dst[at, LANES : LANES + n] = own[frm, :] * jnp.broadcast_to(
                m[:, LANES : LANES + n], (c, n)
            )
            dst[at, :LANES] = xlo_ref[side, :] * jnp.broadcast_to(m[:, :LANES], (c, LANES))
            dst[at, LANES + n :] = xhi_ref[side, :] * jnp.broadcast_to(
                m[:, LANES + n :], (c, LANES)
            )

    m6 = GROUP * c
    for y0 in row_starts(ny):

        @pl.loop(0, nx // 2)
        def _(pair):
            col = pl.multiple_of(pair * 2 * LANES, 2 * LANES)
            pres = conv_rows(w_ref[0], s_in, y0 * c, col, c)
            backs = conv_rows(w_ref[1], s_cot, y0 * c, col, c)
            own = slice(y0 * c, y0 * c + m6)
            for half in range(2):
                v = pres[half] + bias_ref[...]
                s = 0.5 * jnp.tanh(0.5 * v) + 0.5
                at = pl.ds(col + half * LANES, LANES)
                keep = keep_rows(mask_ref, y0 + 1, col + (1 + half) * LANES, c)
                sk = s * keep
                h = v * sk
                g = backs[half] * (sk * (1.0 + v * (1.0 - s)))
                hid[own, at] = h.astype(jnp.bfloat16)
                pre_ref[own, at] = g.astype(jnp.bfloat16)
                for k, step in ((0, -1), (1, 1)):
                    hid_sh[k, own, at] = shifted(h, step).astype(jnp.bfloat16)
                    pre_sh[k, own, at] = shifted(g, step).astype(jnp.bfloat16)

    bias_acc[...] = jnp.zeros_like(bias_acc)

    @pl.loop(0, nx)
    def _(x):
        p = pre_ref[:, pl.ds(pl.multiple_of(x * LANES, LANES), LANES)].astype(jnp.float32)
        bias_acc[...] += jnp.sum(p.reshape(ny, c, LANES), axis=0)

    acc1[...] = jnp.zeros_like(acc1)
    acc2[...] = jnp.zeros_like(acc2)
    wr = WGROUP * c

    def weight_part(acc, p, y, sh, mid, other):
        own = pl.ds(pl.multiple_of(y * c, wr), wr)
        lhs = jnp.concatenate([sh[0, own, :], mid[own, :], sh[1, own, :]], axis=0)
        rhs = other[
            pl.ds(pl.multiple_of(y * c, wr), (WGROUP + 2) * c), p * LANES : p * LANES + n
        ]
        acc[p] += lax.dot_general(
            lhs, rhs, (((1,), (1,)), ((), ())), preferred_element_type=jnp.float32
        )

    @pl.loop(0, ny // WGROUP)
    def _(g):
        y = g * WGROUP
        for p in range(3):
            weight_part(acc1, p, y, pre_sh, pre_ref, s_in)
            weight_part(acc2, p, y, hid_sh, hid, s_cot)

    grad_ref[...] = jnp.zeros_like(grad_ref)
    for which, acc in ((0, acc1), (1, acc2)):
        for p in range(3):
            for r in range(3):
                total = acc[p, r * wr : r * wr + c, 0 : 3 * c]
                for y in range(1, WGROUP):
                    total += acc[p, r * wr + y * c : r * wr + (y + 1) * c, y * c : (y + 3) * c]
                tap = p * 3 + r if which == 0 else 8 - (p * 3 + r)
                base = (which * 9 + tap) * c
                grad_ref[base : base + c, 0 : 3 * c] = total
    bias_col = jnp.sum(bias_acc[...], axis=1, keepdims=True)
    grad_ref[:c, 3 * c :] = jnp.broadcast_to(bias_col, (c, LANES - 3 * c))


def input_kernel(
    channels, ny, nx, pre_ref, sides_ref, ends_ref, mask_ref, w_ref, out_ref, pre
):
    c = channels
    n = nx * LANES
    rows = ny * c
    pre[:c, :] = ends_ref[0]
    pre[c + rows :, :] = ends_ref[1]
    pre[c : c + rows, :LANES] = sides_ref[0]
    pre[c : c + rows, LANES + n :] = sides_ref[1]
    pre[c : c + rows, LANES : LANES + n] = pre_ref[...]
    m6 = GROUP * c
    for y0 in row_starts(ny):

        @pl.loop(0, nx // 2)
        def _(pair):
            col = pl.multiple_of(pair * 2 * LANES, 2 * LANES)
            outs = conv_rows(w_ref[2], pre, y0 * c, col, c)
            for half in range(2):
                keep = keep_rows(mask_ref, y0 + 1, col + (1 + half) * LANES, c)
                out_ref[y0 * c : y0 * c + m6, pl.ds(col + half * LANES, LANES)] = (
                    outs[half] * keep
                ).astype(jnp.bfloat16)


def total_kernel(
    wide, narrow, scale, channels, x_ref, pre_ref, out_ref, sides_ref, ends_ref,
    part, parts_n, parts_w, block, whole, sides, ends,
    s1, r1, s2, r2, s3, r3, s4, r4, sh, rh,
):
    me_w, me_n = lax.axis_index("wide"), lax.axis_index("narrow")

    def send(src, dst, s, r, w, n):
        copy = pltpu.make_async_remote_copy(
            src_ref=src, dst_ref=dst, send_sem=s, recv_sem=r,
            device_id=(w, n), device_id_type=pl.DeviceIdType.MESH,
        )
        copy.start()
        return copy

    barrier = pltpu.get_barrier_semaphore()
    peers_n = [lax.rem(me_n + k, narrow) for k in range(1, narrow)]
    peers_w = [lax.rem(me_w + k, wide) for k in range(1, wide)]
    for n in peers_n:
        pl.semaphore_signal(barrier, inc=1, device_id=(me_w, n), device_id_type=pl.DeviceIdType.MESH)
    for w in peers_w:
        pl.semaphore_signal(barrier, inc=1, device_id=(w, me_n), device_id_type=pl.DeviceIdType.MESH)
    w_up, w_down = lax.rem(me_w + 1, wide), lax.rem(me_w + wide - 1, wide)
    n_up, n_down = lax.rem(me_n + 1, narrow), lax.rem(me_n + narrow - 1, narrow)
    corners = [(w, n) for w in (w_up, w_down) for n in (n_up, n_down)]
    for corner in corners:
        pl.semaphore_signal(barrier, inc=1, device_id=corner, device_id_type=pl.DeviceIdType.MESH)
    pl.semaphore_wait(barrier, len(peers_n) + len(peers_w) + len(corners))

    copies = [
        send(x_ref.at[n], parts_n.at[k], s1.at[k], r1.at[k], me_w, n)
        for k, n in enumerate(peers_n)
    ]
    c = channels
    rows, n = pre_ref.shape
    first, last = pl.ds(0, LANES), pl.ds(n - LANES, LANES)
    top, bottom = pl.ds(0, c), pl.ds(rows - c, c)
    mid, far = pl.ds(LANES, n), pl.ds(LANES + n, LANES)
    halos = [
        (pre_ref.at[:, last], sides.at[0], w_up, me_n),
        (pre_ref.at[:, first], sides.at[1], w_down, me_n),
        (pre_ref.at[bottom, :], ends.at[0, :, mid], me_w, n_up),
        (pre_ref.at[top, :], ends.at[1, :, mid], me_w, n_down),
        (pre_ref.at[bottom, last], ends.at[0, :, first], w_up, n_up),
        (pre_ref.at[bottom, first], ends.at[0, :, far], w_down, n_up),
        (pre_ref.at[top, last], ends.at[1, :, first], w_up, n_down),
        (pre_ref.at[top, first], ends.at[1, :, far], w_down, n_down),
    ]
    halos = [send(src, dst, sh.at[k], rh.at[k], w, m) for k, (src, dst, w, m) in enumerate(halos)]
    for copy in copies:
        copy.wait()
    total = x_ref[me_n]
    for k in range(narrow - 1):
        total += parts_n[k]
    part[...] = total
    copies = [
        send(part.at[w], parts_w.at[k], s2.at[k], r2.at[k], w, me_n)
        for k, w in enumerate(peers_w)
    ]
    for copy in copies:
        copy.wait()
    total = part[me_w]
    for k in range(wide - 1):
        total += parts_w[k]
    block[me_w] = total * scale
    copies = [
        send(block.at[me_w], block.at[me_w], s3.at[k], r3.at[k], w, me_n)
        for k, w in enumerate(peers_w)
    ]
    for copy in copies:
        copy.wait()
    whole[me_n] = block[...]
    copies = [
        send(block, whole.at[me_n], s4.at[k], r4.at[k], me_w, n)
        for k, n in enumerate(peers_n)
    ]
    for copy in copies:
        copy.wait()
    out_ref[...] = whole[...]
    for copy in halos:
        copy.wait()
    outside = ((me_w == 0), (me_w == wide - 1), (me_n == 0), (me_n == narrow - 1))
    w_lo, w_hi, n_lo, n_hi = [jnp.where(end, 0.0, 1.0).astype(jnp.float32) for end in outside]

    def scaled(value, factor):
        return (value.astype(jnp.float32) * factor).astype(value.dtype)

    sides_ref[0] = scaled(sides[0], w_lo)
    sides_ref[1] = scaled(sides[1], w_hi)
    for k, factor in ((0, n_lo), (1, n_hi)):
        ends_ref[k, :, :LANES] = scaled(ends[k, :, :LANES], factor * w_lo)
        ends_ref[k, :, LANES : LANES + n] = scaled(ends[k, :, LANES : LANES + n], factor)
        ends_ref[k, :, LANES + n :] = scaled(ends[k, :, LANES + n :], factor * w_hi)


def total(grads, pre, channels, wide, narrow, scale):
    lanes = grads.shape[-1]
    rows = grads.shape[0] // (wide * narrow)
    vmem = pl.BlockSpec(memory_space=pltpu.VMEM)
    f32 = jnp.float32
    sems = [
        pltpu.SemaphoreType.DMA((count - 1,))
        for count in (narrow, narrow, wide, wide, wide, wide, narrow, narrow)
    ]
    side = jax.ShapeDtypeStruct((2, pre.shape[0], LANES), pre.dtype)
    end = jax.ShapeDtypeStruct((2, channels, pre.shape[1] + 2 * LANES), pre.dtype)
    out, sides, ends = pl.pallas_call(
        functools.partial(total_kernel, wide, narrow, scale, channels),
        out_shape=(jax.ShapeDtypeStruct((narrow, wide, rows, lanes), f32), side, end),
        in_specs=[vmem, vmem],
        out_specs=(vmem, vmem, vmem),
        scratch_shapes=[
            pltpu.VMEM((wide, rows, lanes), f32),
            pltpu.VMEM((narrow - 1, wide, rows, lanes), f32),
            pltpu.VMEM((wide - 1, rows, lanes), f32),
            pltpu.VMEM((wide, rows, lanes), f32),
            pltpu.VMEM((narrow, wide, rows, lanes), f32),
            pltpu.VMEM(side.shape, side.dtype),
            pltpu.VMEM(end.shape, end.dtype),
        ] + sems + [pltpu.SemaphoreType.DMA((8,))] * 2,
        compiler_params=pltpu.CompilerParams(
            collective_id=0, has_side_effects=True, vmem_limit_bytes=32 * 1024 * 1024
        ),
        name="total",
    )(grads.reshape(narrow, wide, rows, lanes), pre)
    return out.reshape(-1, lanes), sides, ends


def body(inputs, cotangent, active_list, conv_first, conv_second, bias_first):
    c, nx, ny, nz = inputs.shape
    depth_blocks = nz // 8
    listing = active_list.reshape(-1)
    ids = jnp.arange(BX * BY * depth_blocks, dtype=jnp.int32)
    present = jnp.any(listing[:, None] == ids[None, :], axis=0).astype(jnp.bfloat16)
    present = present.reshape(BX, BY, depth_blocks).transpose(1, 0, 2)
    mask = jnp.repeat(jnp.repeat(jnp.repeat(present, 8, 2), 8, 1), 8, 0).reshape(ny, nx * nz)

    own_in = inputs.transpose(2, 0, 1, 3).reshape(ny * c, nx * nz)
    own_cot = cotangent.transpose(2, 0, 1, 3).reshape(ny * c, nx * nz)

    def exchange(axis, tail, head):
        count = lax.axis_size(axis)
        lo = lax.ppermute(tail, axis, [(i, i + 1) for i in range(count - 1)])
        hi = lax.ppermute(head, axis, [(i + 1, i) for i in range(count - 1)])
        return lo, hi

    columns = lambda cut: jnp.concatenate([cut(own_in), cut(own_cot), cut(mask)], axis=0)
    xlo, xhi = exchange(
        "wide", columns(lambda a: a[:, -nz:]), columns(lambda a: a[:, :nz])
    )
    n = ny * c

    def rows(first):
        parts = []
        for base, own, per in ((0, own_in, c), (n, own_cot, c), (2 * n, mask, 1)):
            r0 = 0 if first else (ny - 1) * per
            r1 = r0 + per
            parts.append(
                jnp.concatenate(
                    [xlo[base + r0 : base + r1], own[r0:r1], xhi[base + r0 : base + r1]], axis=1
                )
            )
        return jnp.concatenate(parts, axis=0)

    ylo, yhi = exchange("narrow", rows(False), rows(True))
    mask_mid = jnp.concatenate([xlo[2 * n :], mask, xhi[2 * n :]], axis=1)
    full_mask = jnp.concatenate([ylo[2 * c :], mask_mid, yhi[2 * c :]], axis=0)
    full_mask = full_mask.astype(jnp.float32).reshape(ny + 2, 1, (nx + 2) * nz)

    taps = jnp.stack(
        [
            conv_first,
            conv_second[::-1].transpose(0, 2, 1),
            conv_first[::-1].transpose(0, 2, 1),
        ]
    )
    weights = toeplitz(taps, c)
    bias = jnp.broadcast_to(bias_first[None, :, None], (GROUP, c, LANES)).reshape(-1, LANES)

    wide, narrow = lax.axis_size("wide"), lax.axis_size("narrow")
    unit = wide * narrow * 8
    grad_rows = -(-18 * c // unit) * unit
    vmem = pl.BlockSpec(memory_space=pltpu.VMEM)
    bf = jnp.bfloat16
    shape = (ny * c, nx * nz)
    halo_shape = ((ny + 2) * c, (nx + 2) * nz)
    acc_shape = (3, 3 * WGROUP * c, (WGROUP + 2) * c)
    params = pltpu.CompilerParams(vmem_limit_bytes=48 * 1024 * 1024)
    pre, grads = pl.pallas_call(
        functools.partial(grads_kernel, c, ny, nx),
        out_shape=(
            jax.ShapeDtypeStruct(shape, bf),
            jax.ShapeDtypeStruct((grad_rows, LANES), jnp.float32),
        ),
        in_specs=[vmem] * 9,
        out_specs=(vmem, vmem),
        scratch_shapes=[
            pltpu.VMEM(halo_shape, bf),
            pltpu.VMEM(halo_shape, bf),
            pltpu.VMEM(shape, bf),
            pltpu.VMEM((2,) + shape, bf),
            pltpu.VMEM((2,) + shape, bf),
            pltpu.VMEM(acc_shape, jnp.float32),
            pltpu.VMEM(acc_shape, jnp.float32),
            pltpu.VMEM((c, LANES), jnp.float32),
        ],
        compiler_params=params,
        name="local_grads",
    )(own_in, own_cot, full_mask, xlo, xhi, ylo, yhi, weights, bias)

    scale = 1.0 / math.sqrt(nx * wide * ny * narrow * nz)
    grads, sides, ends = total(grads, pre, c, wide, narrow, scale)
    out = pl.pallas_call(
        functools.partial(input_kernel, c, ny, nx),
        out_shape=jax.ShapeDtypeStruct(shape, bf),
        in_specs=[vmem] * 5,
        out_specs=vmem,
        scratch_shapes=[pltpu.VMEM(halo_shape, bf)],
        compiler_params=params,
        name="input_grad",
    )(pre, sides, ends, full_mask, weights)
    input_grad = out.reshape(ny, c, nx, nz).transpose(1, 2, 0, 3)
    both = grads[: 18 * c, : 3 * c].reshape(2, 3, 3, c, 3, c)
    first_grad = both[0].transpose(0, 3, 1, 2, 4).reshape(27, c, c)
    second_grad = both[1][:, :, :, ::-1].transpose(0, 3, 1, 4, 2).reshape(27, c, c)
    return input_grad, first_grad, second_grad, grads[:c, 3 * c]


def solution(mesh):
    return jax.shard_map(
        body,
        mesh=mesh,
        in_specs=(
            P(None, "wide", "narrow", None),
            P(None, "wide", "narrow", None),
            P("wide", "narrow", None),
            P(),
            P(),
            P(),
        ),
        out_specs=(P(None, "wide", "narrow", None), P(), P(), P()),
        check_vma=False,
    )
```

```python
import functools
import math

import jax
import jax.numpy as jnp
from jax import lax
from jax.experimental import pallas as pl
from jax.experimental.pallas import tpu as pltpu
from jax.sharding import PartitionSpec as P

BX = 2
BY = 2
LANES = 128
GROUP = 6
WGROUP = 4


def toeplitz(taps_ref, kind, opposite, dst, channels):
    c = channels
    span = (GROUP + 2) * c
    for p in range(3):
        for r in range(3):
            base = None
            for q in range(3):
                tap = 9 * p + 3 * q + r
                value = taps_ref[kind, 26 - tap if opposite else tap]
                value = jnp.concatenate(
                    [value, jnp.zeros((c, span - LANES), jnp.float32)], axis=1
                )
                base = value if base is None else base + pltpu.roll(value, q * c, 1)
            for y in range(GROUP):
                row = (r * GROUP + y) * c
                moved = pltpu.roll(base, y * c, 1) if y else base
                dst[row : row + c, p * span : (p + 1) * span] = moved.astype(jnp.bfloat16)


def shifted(value, step):
    lane = lax.broadcasted_iota(jnp.int32, value.shape, 1)
    moved = pltpu.roll(value, step % LANES, 1)
    return jnp.where(lane == (0 if step == 1 else LANES - 1), 0.0, moved)


def conv_rows(weights, source, row, col, channels):
    span = (GROUP + 2) * channels
    operand = jnp.concatenate(
        [source[pl.ds(row, span), pl.ds(col + p * LANES, 2 * LANES)] for p in range(3)], axis=0
    )
    out = jnp.dot(weights, operand, preferred_element_type=jnp.float32)
    m = GROUP * channels
    halves = []
    for half in range(2):
        part = out[:, half * LANES : (half + 1) * LANES]
        halves.append(
            shifted(part[:m], 1) + part[m : 2 * m] + shifted(part[2 * m :], -1)
        )
    return halves


def row_starts(ny):
    starts = list(range(0, ny - GROUP + 1, GROUP))
    if starts[-1] + GROUP < ny:
        starts.append(ny - GROUP)
    return starts


def keep_rows(mask_ref, row, col, channels):
    keep = mask_ref[row : row + GROUP, :, pl.ds(col, LANES)]
    return jnp.broadcast_to(keep, (GROUP, channels, LANES)).reshape(GROUP * channels, LANES)


def grads_kernel(
    channels, ny, nx,
    in_ref, cot_ref, mask_ref, xlo_ref, xhi_ref, ylo_ref, yhi_ref, taps_ref, bias_ref,
    pre_ref, grad_ref,
    s_in, s_cot, hid, hid_sh, pre_sh, acc1, acc2, bias_acc, w_ref,
):
    c = channels
    toeplitz(taps_ref, 0, False, w_ref.at[0], c)
    toeplitz(taps_ref, 1, True, w_ref.at[1], c)
    rows = ny * c
    n = nx * LANES
    wide = n + 2 * LANES
    for which, own, dst in ((0, in_ref, s_in), (1, cot_ref, s_cot)):
        for src, at in ((ylo_ref, 0), (yhi_ref, ny + 1)):
            m = jnp.broadcast_to(mask_ref[at].astype(jnp.bfloat16), (c, wide))
            dst[at * c : (at + 1) * c, :] = src[which * c : (which + 1) * c, :] * m

        @pl.loop(0, ny)
        def _(y):
            at = pl.ds(pl.multiple_of((y + 1) * c, c), c)
            frm = pl.ds(pl.multiple_of(y * c, c), c)
            side = pl.ds(pl.multiple_of(which * rows + y * c, c), c)
            m = mask_ref[y + 1].astype(jnp.bfloat16)
            dst[at, LANES : LANES + n] = own[frm, :] * jnp.broadcast_to(
                m[:, LANES : LANES + n], (c, n)
            )
            dst[at, :LANES] = xlo_ref[side, :] * jnp.broadcast_to(m[:, :LANES], (c, LANES))
            dst[at, LANES + n :] = xhi_ref[side, :] * jnp.broadcast_to(
                m[:, LANES + n :], (c, LANES)
            )

    m6 = GROUP * c
    for y0 in row_starts(ny):

        @pl.loop(0, nx // 2)
        def _(pair):
            col = pl.multiple_of(pair * 2 * LANES, 2 * LANES)
            pres = conv_rows(w_ref[0], s_in, y0 * c, col, c)
            backs = conv_rows(w_ref[1], s_cot, y0 * c, col, c)
            own = slice(y0 * c, y0 * c + m6)
            for half in range(2):
                v = pres[half] + bias_ref[...]
                s = 0.5 * jnp.tanh(0.5 * v) + 0.5
                at = pl.ds(col + half * LANES, LANES)
                keep = keep_rows(mask_ref, y0 + 1, col + (1 + half) * LANES, c)
                sk = s * keep
                h = v * sk
                g = backs[half] * (sk * (1.0 + v * (1.0 - s)))
                hid[own, at] = h.astype(jnp.bfloat16)
                pre_ref[own, at] = g.astype(jnp.bfloat16)
                for k, step in ((0, -1), (1, 1)):
                    hid_sh[k, own, at] = shifted(h, step).astype(jnp.bfloat16)
                    pre_sh[k, own, at] = shifted(g, step).astype(jnp.bfloat16)

    bias_acc[...] = jnp.zeros_like(bias_acc)

    @pl.loop(0, nx)
    def _(x):
        p = pre_ref[:, pl.ds(pl.multiple_of(x * LANES, LANES), LANES)].astype(jnp.float32)
        bias_acc[...] += jnp.sum(p.reshape(ny, c, LANES), axis=0)

    acc1[...] = jnp.zeros_like(acc1)
    acc2[...] = jnp.zeros_like(acc2)
    wr = WGROUP * c

    def weight_part(acc, p, y, sh, mid, other):
        own = pl.ds(pl.multiple_of(y * c, wr), wr)
        lhs = jnp.concatenate([sh[0, own, :], mid[own, :], sh[1, own, :]], axis=0)
        rhs = other[
            pl.ds(pl.multiple_of(y * c, wr), (WGROUP + 2) * c), p * LANES : p * LANES + n
        ]
        acc[p] += lax.dot_general(
            lhs, rhs, (((1,), (1,)), ((), ())), preferred_element_type=jnp.float32
        )

    @pl.loop(0, ny // WGROUP)
    def _(g):
        y = g * WGROUP
        for p in range(3):
            weight_part(acc1, p, y, pre_sh, pre_ref, s_in)
            weight_part(acc2, p, y, hid_sh, hid, s_cot)

    grad_ref[...] = jnp.zeros_like(grad_ref)
    for which, acc in ((0, acc1), (1, acc2)):
        for p in range(3):
            for r in range(3):
                total = acc[p, r * wr : r * wr + c, 0 : 3 * c]
                for y in range(1, WGROUP):
                    total += acc[p, r * wr + y * c : r * wr + (y + 1) * c, y * c : (y + 3) * c]
                tap = p * 3 + r if which == 0 else 8 - (p * 3 + r)
                base = (which * 9 + tap) * c
                grad_ref[base : base + c, 0 : 3 * c] = total
    bias_col = jnp.sum(bias_acc[...], axis=1, keepdims=True)
    grad_ref[:c, 3 * c :] = jnp.broadcast_to(bias_col, (c, LANES - 3 * c))


def input_kernel(
    channels, ny, nx, pre_ref, sides_ref, ends_ref, mask_ref, taps_ref, out_ref, pre, w_ref
):
    c = channels
    toeplitz(taps_ref, 2, True, w_ref, c)
    n = nx * LANES
    rows = ny * c
    pre[:c, :] = ends_ref[0]
    pre[c + rows :, :] = ends_ref[1]
    pre[c : c + rows, :LANES] = sides_ref[0]
    pre[c : c + rows, LANES + n :] = sides_ref[1]
    pre[c : c + rows, LANES : LANES + n] = pre_ref[...]
    m6 = GROUP * c
    for y0 in row_starts(ny):

        @pl.loop(0, nx // 2)
        def _(pair):
            col = pl.multiple_of(pair * 2 * LANES, 2 * LANES)
            outs = conv_rows(w_ref[...], pre, y0 * c, col, c)
            for half in range(2):
                keep = keep_rows(mask_ref, y0 + 1, col + (1 + half) * LANES, c)
                out_ref[y0 * c : y0 * c + m6, pl.ds(col + half * LANES, LANES)] = (
                    outs[half] * keep
                ).astype(jnp.bfloat16)


def total_kernel(
    wide, narrow, scale, channels, x_ref, pre_ref, out_ref, sides_ref, ends_ref,
    part, parts_n, parts_w, block, whole, sides, ends,
    s1, r1, s2, r2, s3, r3, s4, r4, sh, rh,
):
    me_w, me_n = lax.axis_index("wide"), lax.axis_index("narrow")

    def send(src, dst, s, r, w, n):
        copy = pltpu.make_async_remote_copy(
            src_ref=src, dst_ref=dst, send_sem=s, recv_sem=r,
            device_id=(w, n), device_id_type=pl.DeviceIdType.MESH,
        )
        copy.start()
        return copy

    barrier = pltpu.get_barrier_semaphore()
    peers_n = [lax.rem(me_n + k, narrow) for k in range(1, narrow)]
    peers_w = [lax.rem(me_w + k, wide) for k in range(1, wide)]
    for n in peers_n:
        pl.semaphore_signal(barrier, inc=1, device_id=(me_w, n), device_id_type=pl.DeviceIdType.MESH)
    for w in peers_w:
        pl.semaphore_signal(barrier, inc=1, device_id=(w, me_n), device_id_type=pl.DeviceIdType.MESH)
    w_up, w_down = lax.rem(me_w + 1, wide), lax.rem(me_w + wide - 1, wide)
    n_up, n_down = lax.rem(me_n + 1, narrow), lax.rem(me_n + narrow - 1, narrow)
    corners = [(w, n) for w in (w_up, w_down) for n in (n_up, n_down)]
    for corner in corners:
        pl.semaphore_signal(barrier, inc=1, device_id=corner, device_id_type=pl.DeviceIdType.MESH)
    pl.semaphore_wait(barrier, len(peers_n) + len(peers_w) + len(corners))

    copies = [
        send(x_ref.at[n], parts_n.at[k], s1.at[k], r1.at[k], me_w, n)
        for k, n in enumerate(peers_n)
    ]
    c = channels
    rows, n = pre_ref.shape
    first, last = pl.ds(0, LANES), pl.ds(n - LANES, LANES)
    top, bottom = pl.ds(0, c), pl.ds(rows - c, c)
    mid, far = pl.ds(LANES, n), pl.ds(LANES + n, LANES)
    halos = [
        (pre_ref.at[:, last], sides.at[0], w_up, me_n),
        (pre_ref.at[:, first], sides.at[1], w_down, me_n),
        (pre_ref.at[bottom, :], ends.at[0, :, mid], me_w, n_up),
        (pre_ref.at[top, :], ends.at[1, :, mid], me_w, n_down),
        (pre_ref.at[bottom, last], ends.at[0, :, first], w_up, n_up),
        (pre_ref.at[bottom, first], ends.at[0, :, far], w_down, n_up),
        (pre_ref.at[top, last], ends.at[1, :, first], w_up, n_down),
        (pre_ref.at[top, first], ends.at[1, :, far], w_down, n_down),
    ]
    halos = [send(src, dst, sh.at[k], rh.at[k], w, m) for k, (src, dst, w, m) in enumerate(halos)]
    for copy in copies:
        copy.wait()
    total = x_ref[me_n]
    for k in range(narrow - 1):
        total += parts_n[k]
    part[...] = total
    copies = [
        send(part.at[w], parts_w.at[k], s2.at[k], r2.at[k], w, me_n)
        for k, w in enumerate(peers_w)
    ]
    for copy in copies:
        copy.wait()
    total = part[me_w]
    for k in range(wide - 1):
        total += parts_w[k]
    block[me_w] = total * scale
    copies = [
        send(block.at[me_w], block.at[me_w], s3.at[k], r3.at[k], w, me_n)
        for k, w in enumerate(peers_w)
    ]
    for copy in copies:
        copy.wait()
    whole[me_n] = block[...]
    copies = [
        send(block, whole.at[me_n], s4.at[k], r4.at[k], me_w, n)
        for k, n in enumerate(peers_n)
    ]
    for copy in copies:
        copy.wait()
    out_ref[...] = whole[...]
    for copy in halos:
        copy.wait()
    outside = ((me_w == 0), (me_w == wide - 1), (me_n == 0), (me_n == narrow - 1))
    w_lo, w_hi, n_lo, n_hi = [jnp.where(end, 0.0, 1.0).astype(jnp.float32) for end in outside]

    def scaled(value, factor):
        return (value.astype(jnp.float32) * factor).astype(value.dtype)

    sides_ref[0] = scaled(sides[0], w_lo)
    sides_ref[1] = scaled(sides[1], w_hi)
    for k, factor in ((0, n_lo), (1, n_hi)):
        ends_ref[k, :, :LANES] = scaled(ends[k, :, :LANES], factor * w_lo)
        ends_ref[k, :, LANES : LANES + n] = scaled(ends[k, :, LANES : LANES + n], factor)
        ends_ref[k, :, LANES + n :] = scaled(ends[k, :, LANES + n :], factor * w_hi)


def total(grads, pre, channels, wide, narrow, scale):
    lanes = grads.shape[-1]
    rows = grads.shape[0] // (wide * narrow)
    vmem = pl.BlockSpec(memory_space=pltpu.VMEM)
    f32 = jnp.float32
    sems = [
        pltpu.SemaphoreType.DMA((count - 1,))
        for count in (narrow, narrow, wide, wide, wide, wide, narrow, narrow)
    ]
    side = jax.ShapeDtypeStruct((2, pre.shape[0], LANES), pre.dtype)
    end = jax.ShapeDtypeStruct((2, channels, pre.shape[1] + 2 * LANES), pre.dtype)
    out, sides, ends = pl.pallas_call(
        functools.partial(total_kernel, wide, narrow, scale, channels),
        out_shape=(jax.ShapeDtypeStruct((narrow, wide, rows, lanes), f32), side, end),
        in_specs=[vmem, vmem],
        out_specs=(vmem, vmem, vmem),
        scratch_shapes=[
            pltpu.VMEM((wide, rows, lanes), f32),
            pltpu.VMEM((narrow - 1, wide, rows, lanes), f32),
            pltpu.VMEM((wide - 1, rows, lanes), f32),
            pltpu.VMEM((wide, rows, lanes), f32),
            pltpu.VMEM((narrow, wide, rows, lanes), f32),
            pltpu.VMEM(side.shape, side.dtype),
            pltpu.VMEM(end.shape, end.dtype),
        ] + sems + [pltpu.SemaphoreType.DMA((8,))] * 2,
        compiler_params=pltpu.CompilerParams(
            collective_id=0, has_side_effects=True, vmem_limit_bytes=32 * 1024 * 1024
        ),
        name="total",
    )(grads.reshape(narrow, wide, rows, lanes), pre)
    return out.reshape(-1, lanes), sides, ends


def body(inputs, cotangent, active_list, conv_first, conv_second, bias_first):
    c, nx, ny, nz = inputs.shape
    depth_blocks = nz // 8
    listing = active_list.reshape(-1)
    ids = jnp.arange(BX * BY * depth_blocks, dtype=jnp.int32)
    present = jnp.any(listing[:, None] == ids[None, :], axis=0).astype(jnp.bfloat16)
    present = present.reshape(BX, BY, depth_blocks).transpose(1, 0, 2)
    mask = jnp.repeat(jnp.repeat(jnp.repeat(present, 8, 2), 8, 1), 8, 0).reshape(ny, nx * nz)

    own_in = inputs.transpose(2, 0, 1, 3).reshape(ny * c, nx * nz)
    own_cot = cotangent.transpose(2, 0, 1, 3).reshape(ny * c, nx * nz)

    def exchange(axis, tail, head):
        count = lax.axis_size(axis)
        lo = lax.ppermute(tail, axis, [(i, i + 1) for i in range(count - 1)])
        hi = lax.ppermute(head, axis, [(i + 1, i) for i in range(count - 1)])
        return lo, hi

    columns = lambda cut: jnp.concatenate([cut(own_in), cut(own_cot), cut(mask)], axis=0)
    xlo, xhi = exchange(
        "wide", columns(lambda a: a[:, -nz:]), columns(lambda a: a[:, :nz])
    )
    n = ny * c

    def rows(first):
        parts = []
        for base, own, per in ((0, own_in, c), (n, own_cot, c), (2 * n, mask, 1)):
            r0 = 0 if first else (ny - 1) * per
            r1 = r0 + per
            parts.append(
                jnp.concatenate(
                    [xlo[base + r0 : base + r1], own[r0:r1], xhi[base + r0 : base + r1]], axis=1
                )
            )
        return jnp.concatenate(parts, axis=0)

    ylo, yhi = exchange("narrow", rows(False), rows(True))
    mask_mid = jnp.concatenate([xlo[2 * n :], mask, xhi[2 * n :]], axis=1)
    full_mask = jnp.concatenate([ylo[2 * c :], mask_mid, yhi[2 * c :]], axis=0)
    full_mask = full_mask.astype(jnp.float32).reshape(ny + 2, 1, (nx + 2) * nz)

    taps = jnp.stack(
        [conv_first, conv_second.transpose(0, 2, 1), conv_first.transpose(0, 2, 1)]
    ).astype(jnp.float32)
    taps = jnp.pad(taps, ((0, 0), (0, 0), (0, 0), (0, LANES - c)))
    matrix = (3 * GROUP * c, 3 * (GROUP + 2) * c)
    bias = jnp.broadcast_to(bias_first[None, :, None], (GROUP, c, LANES)).reshape(-1, LANES)

    wide, narrow = lax.axis_size("wide"), lax.axis_size("narrow")
    unit = wide * narrow * 8
    grad_rows = -(-18 * c // unit) * unit
    vmem = pl.BlockSpec(memory_space=pltpu.VMEM)
    bf = jnp.bfloat16
    shape = (ny * c, nx * nz)
    halo_shape = ((ny + 2) * c, (nx + 2) * nz)
    acc_shape = (3, 3 * WGROUP * c, (WGROUP + 2) * c)
    params = pltpu.CompilerParams(vmem_limit_bytes=48 * 1024 * 1024)
    pre, grads = pl.pallas_call(
        functools.partial(grads_kernel, c, ny, nx),
        out_shape=(
            jax.ShapeDtypeStruct(shape, bf),
            jax.ShapeDtypeStruct((grad_rows, LANES), jnp.float32),
        ),
        in_specs=[vmem] * 9,
        out_specs=(vmem, vmem),
        scratch_shapes=[
            pltpu.VMEM(halo_shape, bf),
            pltpu.VMEM(halo_shape, bf),
            pltpu.VMEM(shape, bf),
            pltpu.VMEM((2,) + shape, bf),
            pltpu.VMEM((2,) + shape, bf),
            pltpu.VMEM(acc_shape, jnp.float32),
            pltpu.VMEM(acc_shape, jnp.float32),
            pltpu.VMEM((c, LANES), jnp.float32),
            pltpu.VMEM((2,) + matrix, bf),
        ],
        compiler_params=params,
        name="local_grads",
    )(own_in, own_cot, full_mask, xlo, xhi, ylo, yhi, taps, bias)

    scale = 1.0 / math.sqrt(nx * wide * ny * narrow * nz)
    grads, sides, ends = total(grads, pre, c, wide, narrow, scale)
    out = pl.pallas_call(
        functools.partial(input_kernel, c, ny, nx),
        out_shape=jax.ShapeDtypeStruct(shape, bf),
        in_specs=[vmem] * 5,
        out_specs=vmem,
        scratch_shapes=[pltpu.VMEM(halo_shape, bf), pltpu.VMEM(matrix, bf)],
        compiler_params=params,
        name="input_grad",
    )(pre, sides, ends, full_mask, taps)
    input_grad = out.reshape(ny, c, nx, nz).transpose(1, 2, 0, 3)
    both = grads[: 18 * c, : 3 * c].reshape(2, 3, 3, c, 3, c)
    first_grad = both[0].transpose(0, 3, 1, 2, 4).reshape(27, c, c)
    second_grad = both[1][:, :, :, ::-1].transpose(0, 3, 1, 4, 2).reshape(27, c, c)
    return input_grad, first_grad, second_grad, grads[:c, 3 * c]


def solution(mesh):
    return jax.shard_map(
        body,
        mesh=mesh,
        in_specs=(
            P(None, "wide", "narrow", None),
            P(None, "wide", "narrow", None),
            P("wide", "narrow", None),
            P(),
            P(),
            P(),
        ),
        out_specs=(P(None, "wide", "narrow", None), P(), P(), P()),
        check_vma=False,
    )
```
